32 devices in a mesh: members: 2 (over x), lon: 16 (over z, y, core).
Axes of the slice: x: 2, y: 2, z: 4, core: 2. Of those that a mesh axis runs over, the one named last changes fastest.
Arguments:
- mesh_latent: bfloat16 [8192, 512], P(('members', 'lon')), parts along dimension 0, may hold values from -6 to 6
- grid_latent: bfloat16 [49152, 512], P(('members', 'lon')), parts along dimension 0, may hold values from -6 to 6
- edge_tiles: bfloat16 [192, 8, 128, 128], P('lon'), may hold values from -0.1875 to 0.1875
- sender_ids: int32 [192, 8], P('lon'), may hold values from 0 to 31, as said below
- block_count: int32 [192], P('lon'), may hold values from 1 to 8, as said below
- w_send: bfloat16 [512, 512], replicated, may hold values from -0.25 to 0.25
- w_grid: bfloat16 [512, 512], replicated, may hold values from -0.25 to 0.25
- w_agg: bfloat16 [512, 512], replicated, may hold values from -0.25 to 0.25
- w_out: bfloat16 [83, 512], replicated, may hold values from -0.25 to 0.25
- cotangent: bfloat16 [166, 24576], P('members', 'lon'), parts along dimension 0, may hold values from -6 to 6
Outputs:
- predictions: float32 [166, 24576], P('members', 'lon'), parts along dimension 0
- grad_mesh: float32 [8192, 512], P(('members', 'lon')), parts along dimension 0
- grad_grid: float32 [49152, 512], P(('members', 'lon')), parts along dimension 0
The draws below stay inside these ranges and needn't reach their ends.
There are 2 independent parts, one for each index of `members`. The reference program is written for one: setup_inputs(seed, part) draws one part's arguments, and reference() takes and returns one part's arrays. A program takes and returns all parts, laid end to end along the dimension named above; an argument that names none is the same for every part. Nothing has to cross between parts.
Inputs may be any that keep to these rules, and one draw needn't show every extreme that they name: sender_ids[r, k] names a mesh block of the index of lon that holds receiver block r or of one of its two neighbours on the loop: ((r // 12 + j) * 2 + i) mod 32 with j in -1, 0, 1 and 0 <= i < 2; in slot 0, j is -1 for the first receiver block of each index of lon and +1 for the second. `block_count`: some receiver block uses all 8 slots.
All inputs are finite; a program needn't handle non-finite values.
Results may differ from the reference program's by a relative error of at most 0.0055.
Values may be sent and summed in bfloat16 or wider, within the bound.
A program may use at most 128 MiB of HBM per device.

```python
import jax
import jax.numpy as jnp
from jax import lax

D = 512
VARS = 83
BLK = 128
EB = 8
MB_DEV = 2
RB_DEV = 12
MBLOCKS = 32
MESH = 4096
RBLOCKS = 192
GRID = 24576


def draw_sender_ids(key, part):
    key = jax.random.fold_in(key, 11)
    first, second = jax.random.split(key)
    offset = jax.random.randint(first, (RBLOCKS, EB), -1, 2)
    local = jnp.arange(RBLOCKS, dtype=jnp.int32) % RB_DEV
    forced = jnp.where(local == 0, -1, jnp.where(local == 1, 1, offset[:, 0]))
    offset = offset.at[:, 0].set(forced.astype(jnp.int32))
    within = jax.random.randint(second, (RBLOCKS, EB), 0, MB_DEV)
    owner = (jnp.arange(RBLOCKS, dtype=jnp.int32) // RB_DEV)[:, None]
    return jnp.mod((owner + offset) * MB_DEV + within, MBLOCKS).astype(jnp.int32)


def draw_block_count(key, part):
    key = jax.random.fold_in(key, 23)
    first, second = jax.random.split(key)
    counts = jax.random.randint(first, (RBLOCKS,), 1, EB + 1)
    place = jax.random.randint(second, (), 0, RBLOCKS)
    return counts.at[place].set(EB).astype(jnp.int32)


def shard_levels(key, extent, cuts, smallest, high):
    loudness = 1.0
    for axis_at, shards_of in cuts:
        heights = jax.random.uniform(jax.random.fold_in(jax.random.fold_in(key, 6), axis_at), (shards_of,), jnp.float32, smallest / len(cuts), high / len(cuts))
        loudness = loudness * jnp.repeat(jnp.exp(heights), extent[axis_at] // shards_of).reshape((-1,) + (1,) * (len(extent) - 1 - axis_at))
    return loudness


def bell_draw(stream_key, dims, deviation, limit, shards=(), held_as=jnp.bfloat16):
    entries = deviation * jax.random.normal(stream_key, dims, jnp.float32)
    if shards:
        entries = entries * shard_levels(stream_key, dims, shards, -0.22, 0.18)
    return jnp.clip(entries, -limit, limit).astype(held_as)


def setup_inputs(seed: int = 0, part: int = 0) -> dict:
    seeds = jax.random.split(jax.random.key(seed), 11)
    own_keys = jax.random.split(jax.random.fold_in(seeds[10], part), 11)
    return {
        "mesh_latent": bell_draw(own_keys[0], (MESH, D), 1.0, 6.0, ((0, 16),)),
        "grid_latent": bell_draw(own_keys[1], (GRID, D), 1.0, 6.0, ((0, 16),)),
        "edge_tiles": bell_draw(seeds[2], (RBLOCKS, EB, BLK, BLK), (BLK * EB) ** -0.5, 0.1875, ((0, 16),)),
        "sender_ids": draw_sender_ids(jax.random.fold_in(seeds[10], 71), part),
        "block_count": draw_block_count(jax.random.fold_in(seeds[10], 71), part),
        "w_send": bell_draw(seeds[5], (D, D), D ** -0.5, 0.25),
        "w_grid": bell_draw(seeds[6], (D, D), D ** -0.5, 0.25),
        "w_agg": bell_draw(seeds[7], (D, D), D ** -0.5, 0.25),
        "w_out": bell_draw(seeds[8], (VARS, D), D ** -0.5, 0.25),
        "cotangent": bell_draw(own_keys[9], (VARS, GRID), 1.0, 6.0, ((1, 16),)),
    }


def silu_grad(value):
    gate = jax.nn.sigmoid(value)
    return gate * (1.0 + value * (1.0 - gate))

def reference(mesh_latent, grid_latent, edge_tiles, sender_ids, block_count, w_send, w_grid, w_agg, w_out, cotangent):
    mesh_pre = jnp.dot(mesh_latent, w_send, preferred_element_type=jnp.float32)
    sender = jax.nn.silu(mesh_pre).astype(jnp.bfloat16)
    sender_blocks = sender.reshape(MBLOCKS, BLK, D)
    live = jnp.arange(EB, dtype=jnp.int32)[None, :] < block_count[:, None]
    live_tiles = jnp.where(live[:, :, None, None], edge_tiles, jnp.zeros((), edge_tiles.dtype))

    def one_block(args):
        tiles, ids = args
        picked = jnp.take(sender_blocks, ids.astype(jnp.int32), axis=0)
        return jnp.einsum('kab,kbd->ad', tiles.astype(jnp.float32), picked.astype(jnp.float32)).astype(jnp.bfloat16)
    aggregated = lax.map(one_block, (live_tiles, sender_ids)).reshape(GRID, D)
    pre = jnp.dot(grid_latent, w_grid, preferred_element_type=jnp.float32) + jnp.dot(aggregated, w_agg, preferred_element_type=jnp.float32)
    hidden = jax.nn.silu(pre).astype(jnp.bfloat16)
    predictions = lax.dot_general(w_out, hidden, (((1,), (1,)), ((), ())), preferred_element_type=jnp.float32)
    d_hidden = lax.dot_general(cotangent, w_out, (((0,), (0,)), ((), ())), preferred_element_type=jnp.float32)
    d_pre = (d_hidden * silu_grad(pre)).astype(jnp.bfloat16)
    grad_grid = lax.dot_general(d_pre, w_grid, (((1,), (1,)), ((), ())), preferred_element_type=jnp.float32)
    d_agg = lax.dot_general(d_pre, w_agg, (((1,), (1,)), ((), ())), preferred_element_type=jnp.float32).astype(jnp.bfloat16)
    d_agg_blocks = d_agg.reshape(RBLOCKS, BLK, D)

    def accumulate(carry, args):
        tiles, ids, grad_block = args
        pieces = jnp.einsum('kab,ad->kbd', tiles.astype(jnp.float32), grad_block.astype(jnp.float32))
        return (carry.at[ids.astype(jnp.int32)].add(pieces), None)
    start = jnp.zeros((MBLOCKS, BLK, D), jnp.float32)
    d_sender, _ = lax.scan(accumulate, start, (live_tiles, sender_ids, d_agg_blocks))
    d_sender = d_sender.reshape(MESH, D)
    d_mesh_pre = (d_sender * silu_grad(mesh_pre)).astype(jnp.bfloat16)
    grad_mesh = lax.dot_general(d_mesh_pre, w_send, (((1,), (1,)), ((), ())), preferred_element_type=jnp.float32)
    return (predictions, grad_mesh, grad_grid)
```

```python
import functools

import jax
import jax.numpy as jnp
from jax import lax
from jax.experimental import pallas as pl
from jax.experimental.pallas import tpu as pltpu
from jax.sharding import PartitionSpec as P

MESH = pl.DeviceIdType.MESH
F32 = jnp.float32
BF16 = jnp.bfloat16


def gate_of(value):
    return 0.5 * jnp.tanh(0.5 * value) + 0.5


def matmul(a, b):
    return jnp.dot(a, b, preferred_element_type=F32)


def kernel(
    lanes,
    ids_ref,
    count_ref,
    mesh_hbm,
    grid_hbm,
    tiles_hbm,
    w_send_hbm,
    w_grid_hbm,
    w_agg_hbm,
    w_out_hbm,
    cot_hbm,
    pred_hbm,
    gmesh_hbm,
    ggrid_hbm,
    mesh_v,
    grid_v,
    tiles_v,
    w_send_v,
    w_grid_v,
    w_agg_v,
    w_out_v,
    cot_v,
    w_send_t,
    w_grid_t,
    w_agg_t,
    mesh_pre_v,
    wide_v,
    dense_v,
    dense_t,
    part_v,
    pre_v,
    dhid_v,
    hidden_v,
    dpre_v,
    dagg_v,
    own_v,
    tx_v,
    rx_v,
    pred_v,
    gmesh_v,
    ggrid_v,
    in_sem,
    grid_sem,
    tile_sem,
    out_sem,
    gout_sem,
    fsend_sem,
    frecv_sem,
    bsend_sem,
    brecv_sem,
):
    me = lax.axis_index("lon")
    right, left = lax.rem(me + 1, lanes), lax.rem(me + lanes - 1, lanes)
    rows = mesh_v.shape[0]
    recv, slots, side, _ = tiles_v.shape
    grid_rows = grid_v.shape[0]
    own = rows // side
    total = own * lanes
    chunk = 2 * side
    chunks = grid_rows // chunk
    big = 4 * side
    bigs = grid_rows // big

    barrier = pltpu.get_barrier_semaphore()
    for neighbour in (left, right):
        pl.semaphore_signal(barrier, inc=1, device_id={"lon": neighbour}, device_id_type=MESH)

    def load(at, src, dst):
        return pltpu.make_async_copy(src, dst, in_sem.at[at])

    loads = [
        load(0, mesh_hbm, mesh_v),
        load(1, w_send_hbm, w_send_v),
        load(2, w_grid_hbm, w_grid_v),
        load(3, w_agg_hbm, w_agg_v),
        load(4, w_out_hbm, w_out_v),
        load(5, cot_hbm, cot_v),
    ]

    def grid_copy(c):
        at = pl.ds(c * chunk, chunk)
        return pltpu.make_async_copy(grid_hbm.at[at], grid_v.at[at], grid_sem.at[c])

    def tile_copy(c):
        at = pl.ds(c * 2, 2)
        return pltpu.make_async_copy(tiles_hbm.at[at], tiles_v.at[at], tile_sem.at[c])

    for c in loads:
        c.start()
    for c in range(chunks):
        grid_copy(c).start()
        tile_copy(c).start()

    loads[0].wait()
    loads[1].wait()
    mesh_pre = matmul(mesh_v[...], w_send_v[...])
    mesh_pre_v[...] = mesh_pre
    wide_v[pl.ds(rows, rows), :] = (mesh_pre * gate_of(mesh_pre)).astype(BF16)

    pl.semaphore_wait(barrier, 2)

    def halo(way):
        target, dst = (right, 0) if way == 0 else (left, 2 * rows)
        return pltpu.make_async_remote_copy(
            src_ref=wide_v.at[pl.ds(rows, rows)],
            dst_ref=wide_v.at[pl.ds(dst, rows)],
            send_sem=fsend_sem.at[way],
            recv_sem=frecv_sem.at[way],
            device_id={"lon": target},
            device_id_type=MESH,
        )

    halos = [halo(0), halo(1)]
    for copy in halos:
        copy.start()

    w_send_t[...] = w_send_v[...].T
    for c in loads[2:]:
        c.wait()
    w_grid_t[...] = w_grid_v[...].T
    w_agg_t[...] = w_agg_v[...].T

    sub = 32

    def early(c, carry):
        grid_copy(c).wait()
        tile_copy(c).wait()
        at = pl.ds(pl.multiple_of(c * chunk, chunk), chunk)
        for q in range(2):
            r = c * 2 + q
            rel = []
            for k in range(slots):
                raw = lax.rem(ids_ref[r, k] - me * own + own + total, total)
                rel.append(jnp.where(k < count_ref[r], raw, -1))
            row0 = pl.multiple_of(r * side, side)
            for s in range(side // sub):
                sums = [None] * (3 * own)
                for k in range(slots):
                    tile = tiles_v[r, k, pl.ds(s * sub, sub), :].astype(F32)
                    for j in range(3 * own):
                        term = tile * jnp.where(rel[k] == j, 1.0, 0.0).astype(F32)
                        sums[j] = term if sums[j] is None else sums[j] + term
                for j in range(3 * own):
                    dense_v[pl.ds(row0 + s * sub, sub), j * side : (j + 1) * side] = sums[
                        j
                    ].astype(BF16)
            for j in range(3 * own):
                block = dense_v[pl.ds(row0, side), j * side : (j + 1) * side]
                dense_t[j * side : (j + 1) * side, pl.ds(row0, side)] = block.T
        pre_v[at, :] = matmul(grid_v[at, :], w_grid_v[...])
        dhid_v[at, :] = lax.dot_general(
            cot_v[:, at], w_out_v[...], (((0,), (0,)), ((), ())), preferred_element_type=F32
        )
        part_v[at, :] = matmul(dense_v[at, rows : 2 * rows], wide_v[rows : 2 * rows, :])
        return carry

    lax.fori_loop(0, chunks, early, 0)

    for copy in halos:
        copy.wait_recv()

    def middle(c, carry):
        at = pl.ds(pl.multiple_of(c * big, big), big)
        agg = part_v[at, :] + matmul(dense_v[at, :rows], wide_v[:rows, :])
        agg = agg + matmul(dense_v[at, 2 * rows :], wide_v[2 * rows :, :])
        pre = pre_v[at, :] + matmul(agg.astype(BF16), w_agg_v[...])
        gate = gate_of(pre)
        hidden_v[at, :] = (pre * gate).astype(BF16)
        d_pre = (dhid_v[at, :] * (gate * (1.0 + pre * (1.0 - gate)))).astype(BF16)
        dpre_v[at, :] = d_pre
        dagg_v[at, :] = matmul(d_pre, w_agg_t[...]).astype(BF16)
        return carry

    lax.fori_loop(0, bigs, middle, 0)

    def rim(way):
        target = left if way == 0 else right
        return pltpu.make_async_remote_copy(
            src_ref=tx_v.at[way],
            dst_ref=rx_v.at[way],
            send_sem=bsend_sem.at[way],
            recv_sem=brecv_sem.at[way],
            device_id={"lon": target},
            device_id_type=MESH,
        )

    rims = [rim(0), rim(1)]
    for way, start in ((0, 0), (1, 2 * rows)):
        tx_v[way] = matmul(dense_t[start : start + rows, :], dagg_v[...]).astype(BF16)
        rims[way].start()
    own_v[...] = matmul(dense_t[rows : 2 * rows, :], dagg_v[...])

    def ggrid_copy(c):
        at = pl.ds(c * big, big)
        return pltpu.make_async_copy(ggrid_v.at[at], ggrid_hbm.at[at], gout_sem.at[c])

    def late(c, carry):
        at = pl.ds(pl.multiple_of(c * big, big), big)
        ggrid_v[at, :] = matmul(dpre_v[at, :], w_grid_t[...])
        ggrid_copy(c).start()
        pred_v[:, at] = lax.dot_general(
            w_out_v[...], hidden_v[at, :], (((1,), (1,)), ((), ())), preferred_element_type=F32
        )
        return carry

    lax.fori_loop(0, bigs, late, 0)
    pred_copy = pltpu.make_async_copy(pred_v, pred_hbm, out_sem.at[0])
    pred_copy.start()

    mesh_pre = mesh_pre_v[...]
    gate = gate_of(mesh_pre)
    slope = gate * (1.0 + mesh_pre * (1.0 - gate))
    for copy in rims:
        copy.wait_recv()
    d_sender = own_v[...] + (rx_v[0].astype(F32) + rx_v[1].astype(F32))
    gmesh_v[...] = matmul((d_sender * slope).astype(BF16), w_send_t[...])
    gmesh_copy = pltpu.make_async_copy(gmesh_v, gmesh_hbm, out_sem.at[1])
    gmesh_copy.start()

    for copy in halos + rims:
        copy.wait_send()
    for c in range(bigs):
        ggrid_copy(c).wait()
    pred_copy.wait()
    gmesh_copy.wait()


def per_device(
    mesh_latent,
    grid_latent,
    edge_tiles,
    sender_ids,
    block_count,
    w_send,
    w_grid,
    w_agg,
    w_out,
    cotangent,
):
    lanes = lax.axis_size("lon")
    rows, width = mesh_latent.shape
    grid_rows = grid_latent.shape[0]
    recv, _, side, _ = edge_tiles.shape
    variables = w_out.shape[0]
    wide = 3 * rows
    anywhere = pl.BlockSpec(memory_space=pl.ANY)
    scalars = pl.BlockSpec(memory_space=pltpu.SMEM)
    chunks = recv // 2
    bigs = recv // 4

    def vmem(*shape, dtype=BF16):
        return pltpu.VMEM(shape, dtype)

    square = (width, width)
    return pl.pallas_call(
        functools.partial(kernel, lanes),
        out_shape=(
            jax.ShapeDtypeStruct((variables, grid_rows), F32),
            jax.ShapeDtypeStruct((rows, width), F32),
            jax.ShapeDtypeStruct((grid_rows, width), F32),
        ),
        in_specs=[scalars] * 2 + [anywhere] * 8,
        out_specs=(anywhere,) * 3,
        scratch_shapes=[
            vmem(rows, width),
            vmem(grid_rows, width),
            vmem(*edge_tiles.shape),
            vmem(*square),
            vmem(*square),
            vmem(*square),
            vmem(variables, width),
            vmem(variables, grid_rows),
            vmem(*square),
            vmem(*square),
            vmem(*square),
            vmem(rows, width, dtype=F32),
            vmem(wide, width),
            vmem(grid_rows, wide),
            vmem(wide, grid_rows),
            vmem(grid_rows, width, dtype=F32),
            vmem(grid_rows, width, dtype=F32),
            vmem(grid_rows, width, dtype=F32),
            vmem(grid_rows, width),
            vmem(grid_rows, width),
            vmem(grid_rows, width),
            vmem(rows, width, dtype=F32),
            vmem(2, rows, width),
            vmem(2, rows, width),
            vmem(variables, grid_rows, dtype=F32),
            vmem(rows, width, dtype=F32),
            vmem(grid_rows, width, dtype=F32),
            pltpu.SemaphoreType.DMA((6,)),
            pltpu.SemaphoreType.DMA((chunks,)),
            pltpu.SemaphoreType.DMA((chunks,)),
            pltpu.SemaphoreType.DMA((2,)),
            pltpu.SemaphoreType.DMA((bigs,)),
            pltpu.SemaphoreType.DMA((2,)),
            pltpu.SemaphoreType.DMA((2,)),
            pltpu.SemaphoreType.DMA((2,)),
            pltpu.SemaphoreType.DMA((2,)),
        ],
        compiler_params=pltpu.CompilerParams(
            collective_id=0, has_side_effects=True, vmem_limit_bytes=56 * 2**20
        ),
        cost_estimate=pl.CostEstimate(
            flops=7_000_000_000, bytes_accessed=11_000_000, transcendentals=1_000_000
        ),
    )(
        sender_ids,
        block_count,
        mesh_latent,
        grid_latent,
        edge_tiles,
        w_send,
        w_grid,
        w_agg,
        w_out,
        cotangent,
    )


def solution(mesh):
    placed = (
        P(("members", "lon"), None),
        P(("members", "lon"), None),
        P("lon", None, None, None),
        P("lon", None),
        P("lon"),
        P(),
        P(),
        P(),
        P(),
        P("members", "lon"),
    )
    return jax.shard_map(
        per_device,
        mesh=mesh,
        in_specs=placed,
        out_specs=(P("members", "lon"), P(("members", "lon"), None), P(("members", "lon"), None)),
        check_vma=False,
    )
```

```python
import functools

import jax
import jax.numpy as jnp
from jax import lax
from jax.experimental import pallas as pl
from jax.experimental.pallas import tpu as pltpu
from jax.sharding import PartitionSpec as P

MESH = pl.DeviceIdType.MESH
F32 = jnp.float32
BF16 = jnp.bfloat16


def gate_of(value):
    return 0.5 * jnp.tanh(0.5 * value) + 0.5


def matmul(a, b):
    return jnp.dot(a, b, preferred_element_type=F32)


def kernel(
    lanes,
    ids_ref,
    count_ref,
    mesh_hbm,
    grid_hbm,
    tiles_hbm,
    w_send_hbm,
    w_grid_hbm,
    w_agg_hbm,
    w_out_hbm,
    cot_hbm,
    pred_hbm,
    dmesh_hbm,
    dpre_hbm,
    mesh_v,
    grid_v,
    tiles_v,
    w_send_v,
    w_grid_v,
    w_agg_v,
    w_out_v,
    cot_v,
    w_agg_t,
    mesh_pre_v,
    wide_v,
    dense_v,
    dense_t,
    part_v,
    pre_v,
    dhid_v,
    hidden_v,
    dpre_v,
    dagg_v,
    own_v,
    tx_v,
    rx_v,
    pred_v,
    dmesh_v,
    in_sem,
    grid_sem,
    tile_sem,
    out_sem,
    gout_sem,
    fsend_sem,
    frecv_sem,
    bsend_sem,
    brecv_sem,
):
    me = lax.axis_index("lon")
    right, left = lax.rem(me + 1, lanes), lax.rem(me + lanes - 1, lanes)
    rows = mesh_v.shape[0]
    recv, slots, side, _ = tiles_v.shape
    grid_rows = grid_v.shape[0]
    own = rows // side
    total = own * lanes
    chunk = 2 * side
    chunks = grid_rows // chunk
    big = 4 * side
    bigs = grid_rows // big

    barrier = pltpu.get_barrier_semaphore()
    for neighbour in (left, right):
        pl.semaphore_signal(barrier, inc=1, device_id={"lon": neighbour}, device_id_type=MESH)

    def load(at, src, dst):
        return pltpu.make_async_copy(src, dst, in_sem.at[at])

    loads = [
        load(0, mesh_hbm, mesh_v),
        load(1, w_send_hbm, w_send_v),
        load(2, w_grid_hbm, w_grid_v),
        load(3, w_agg_hbm, w_agg_v),
        load(4, w_out_hbm, w_out_v),
        load(5, cot_hbm, cot_v),
    ]

    def grid_copy(c):
        at = pl.ds(c * chunk, chunk)
        return pltpu.make_async_copy(grid_hbm.at[at], grid_v.at[at], grid_sem.at[c])

    def tile_copy(c):
        at = pl.ds(c * 2, 2)
        return pltpu.make_async_copy(tiles_hbm.at[at], tiles_v.at[at], tile_sem.at[c])

    for c in loads:
        c.start()
    for c in range(chunks):
        grid_copy(c).start()
        tile_copy(c).start()

    loads[0].wait()
    loads[1].wait()
    mesh_pre = matmul(mesh_v[...], w_send_v[...])
    mesh_pre_v[...] = mesh_pre
    wide_v[pl.ds(rows, rows), :] = (mesh_pre * gate_of(mesh_pre)).astype(BF16)

    pl.semaphore_wait(barrier, 2)

    def halo(way):
        target, dst = (right, 0) if way == 0 else (left, 2 * rows)
        return pltpu.make_async_remote_copy(
            src_ref=wide_v.at[pl.ds(rows, rows)],
            dst_ref=wide_v.at[pl.ds(dst, rows)],
            send_sem=fsend_sem.at[way],
            recv_sem=frecv_sem.at[way],
            device_id={"lon": target},
            device_id_type=MESH,
        )

    halos = [halo(0), halo(1)]
    for copy in halos:
        copy.start()

    for c in loads[2:]:
        c.wait()
    w_agg_t[...] = w_agg_v[...].T

    sub = 32

    def early(c, carry):
        grid_copy(c).wait()
        tile_copy(c).wait()
        at = pl.ds(pl.multiple_of(c * chunk, chunk), chunk)
        for q in range(2):
            r = c * 2 + q
            rel = []
            for k in range(slots):
                raw = lax.rem(ids_ref[k, r] - me * own + own + total, total)
                rel.append(jnp.where(k < count_ref[r], raw, -1))
            row0 = pl.multiple_of(r * side, side)
            for s in range(side // sub):
                sums = [None] * (3 * own)
                for k in range(slots):
                    tile = tiles_v[r, k, pl.ds(s * sub, sub), :].astype(F32)
                    for j in range(3 * own):
                        term = tile * jnp.where(rel[k] == j, 1.0, 0.0).astype(F32)
                        sums[j] = term if sums[j] is None else sums[j] + term
                for j in range(3 * own):
                    dense_v[pl.ds(row0 + s * sub, sub), j * side : (j + 1) * side] = sums[
                        j
                    ].astype(BF16)
            for j in range(3 * own):
                block = dense_v[pl.ds(row0, side), j * side : (j + 1) * side]
                dense_t[j * side : (j + 1) * side, pl.ds(row0, side)] = block.T
        pre_v[at, :] = matmul(grid_v[at, :], w_grid_v[...])
        dhid_v[at, :] = lax.dot_general(
            cot_v[:, at], w_out_v[...], (((0,), (0,)), ((), ())), preferred_element_type=F32
        )
        part_v[at, :] = matmul(dense_v[at, rows : 2 * rows], wide_v[rows : 2 * rows, :])
        return carry

    lax.fori_loop(0, chunks, early, 0)

    for copy in halos:
        copy.wait_recv()

    def dpre_copy(c):
        at = pl.ds(c * big, big)
        return pltpu.make_async_copy(dpre_v.at[at], dpre_hbm.at[at], gout_sem.at[c])

    def middle(c, carry):
        at = pl.ds(pl.multiple_of(c * big, big), big)
        agg = part_v[at, :] + matmul(dense_v[at, :rows], wide_v[:rows, :])
        agg = agg + matmul(dense_v[at, 2 * rows :], wide_v[2 * rows :, :])
        pre = pre_v[at, :] + matmul(agg.astype(BF16), w_agg_v[...])
        gate = gate_of(pre)
        hidden_v[at, :] = (pre * gate).astype(BF16)
        d_pre = (dhid_v[at, :] * (gate * (1.0 + pre * (1.0 - gate)))).astype(BF16)
        dpre_v[at, :] = d_pre
        dpre_copy(c).start()
        dagg_v[at, :] = matmul(d_pre, w_agg_t[...]).astype(BF16)
        return carry

    lax.fori_loop(0, bigs, middle, 0)

    def rim(way):
        target = left if way == 0 else right
        return pltpu.make_async_remote_copy(
            src_ref=tx_v.at[way],
            dst_ref=rx_v.at[way],
            send_sem=bsend_sem.at[way],
            recv_sem=brecv_sem.at[way],
            device_id={"lon": target},
            device_id_type=MESH,
        )

    rims = [rim(0), rim(1)]
    for way, start in ((0, 0), (1, 2 * rows)):
        tx_v[way] = matmul(dense_t[start : start + rows, :], dagg_v[...]).astype(BF16)
        rims[way].start()
    own_v[...] = matmul(dense_t[rows : 2 * rows, :], dagg_v[...])

    def late(c, carry):
        at = pl.ds(pl.multiple_of(c * big, big), big)
        pred_v[:, at] = lax.dot_general(
            w_out_v[...], hidden_v[at, :], (((1,), (1,)), ((), ())), preferred_element_type=F32
        )
        return carry

    lax.fori_loop(0, bigs, late, 0)
    pred_copy = pltpu.make_async_copy(pred_v, pred_hbm, out_sem.at[0])
    pred_copy.start()

    mesh_pre = mesh_pre_v[...]
    gate = gate_of(mesh_pre)
    slope = gate * (1.0 + mesh_pre * (1.0 - gate))
    for copy in rims:
        copy.wait_recv()
    d_sender = own_v[...] + (rx_v[0].astype(F32) + rx_v[1].astype(F32))
    dmesh_v[...] = (d_sender * slope).astype(BF16)
    dmesh_copy = pltpu.make_async_copy(dmesh_v, dmesh_hbm, out_sem.at[1])
    dmesh_copy.start()

    for copy in halos + rims:
        copy.wait_send()
    for c in range(bigs):
        dpre_copy(c).wait()
    pred_copy.wait()
    dmesh_copy.wait()


def finish(
    pred_hbm,
    dmesh_hbm,
    dpre_hbm,
    w_send_hbm,
    w_grid_hbm,
    pred_out,
    gmesh_out,
    ggrid_out,
    pred_v,
    dmesh_v,
    dpre_v,
    w_send_v,
    w_grid_v,
    w_grid_t,
    gmesh_v,
    ggrid_v,
    in_sem,
    dpre_sem,
    out_sem,
    gout_sem,
):
    last = (((1,), (1,)), ((), ()))
    parts = dpre_sem.shape[0]
    step = dpre_v.shape[0] // parts

    w_grid_copy = pltpu.make_async_copy(w_grid_hbm, w_grid_v, in_sem.at[0])
    dmesh_copy = pltpu.make_async_copy(dmesh_hbm, dmesh_v, in_sem.at[1])
    w_send_copy = pltpu.make_async_copy(w_send_hbm, w_send_v, in_sem.at[2])
    pred_read = pltpu.make_async_copy(pred_hbm, pred_v, in_sem.at[3])
    pred_copy = pltpu.make_async_copy(pred_v, pred_out, out_sem.at[0])
    gmesh_copy = pltpu.make_async_copy(gmesh_v, gmesh_out, out_sem.at[1])
    reads, writes = [], []
    for c in range(parts):
        at = pl.ds(c * step, step)
        reads.append(pltpu.make_async_copy(dpre_hbm.at[at], dpre_v.at[at], dpre_sem.at[c]))
        writes.append(pltpu.make_async_copy(ggrid_v.at[at], ggrid_out.at[at], gout_sem.at[c]))
    w_grid_copy.start()
    for copy in reads:
        copy.start()
    dmesh_copy.start()
    w_send_copy.start()
    pred_read.start()
    w_grid_copy.wait()
    w_grid_t[...] = w_grid_v[...].T
    for c in range(parts):
        at = pl.ds(c * step, step)
        reads[c].wait()
        ggrid_v[at, :] = matmul(dpre_v[at, :], w_grid_t[...])
        writes[c].start()
    pred_read.wait()
    pred_copy.start()
    dmesh_copy.wait()
    w_send_copy.wait()
    gmesh_v[...] = lax.dot_general(dmesh_v[...], w_send_v[...], last, preferred_element_type=F32)
    gmesh_copy.start()
    for copy in writes:
        copy.wait()
    pred_copy.wait()
    gmesh_copy.wait()


def per_device(
    mesh_latent,
    grid_latent,
    edge_tiles,
    sender_ids,
    block_count,
    w_send,
    w_grid,
    w_agg,
    w_out,
    cotangent,
):
    lanes = lax.axis_size("lon")
    rows, width = mesh_latent.shape
    grid_rows = grid_latent.shape[0]
    recv, _, side, _ = edge_tiles.shape
    variables = w_out.shape[0]
    wide = 3 * rows
    anywhere = pl.BlockSpec(memory_space=pl.ANY)
    scalars = pl.BlockSpec(memory_space=pltpu.SMEM)
    chunks = recv // 2
    bigs = recv // 4

    def vmem(*shape, dtype=BF16):
        return pltpu.VMEM(shape, dtype)

    square = (width, width)
    predictions, d_mesh_pre, d_pre = pl.pallas_call(
        functools.partial(kernel, lanes),
        out_shape=(
            jax.ShapeDtypeStruct((variables, grid_rows), F32),
            jax.ShapeDtypeStruct((rows, width), BF16),
            jax.ShapeDtypeStruct((grid_rows, width), BF16),
        ),
        in_specs=[scalars] * 2 + [anywhere] * 8,
        out_specs=(anywhere,) * 3,
        scratch_shapes=[
            vmem(rows, width),
            vmem(grid_rows, width),
            vmem(*edge_tiles.shape),
            vmem(*square),
            vmem(*square),
            vmem(*square),
            vmem(variables, width),
            vmem(variables, grid_rows),
            vmem(*square),
            vmem(rows, width, dtype=F32),
            vmem(wide, width),
            vmem(grid_rows, wide),
            vmem(wide, grid_rows),
            vmem(grid_rows, width, dtype=F32),
            vmem(grid_rows, width, dtype=F32),
            vmem(grid_rows, width, dtype=F32),
            vmem(grid_rows, width),
            vmem(grid_rows, width),
            vmem(grid_rows, width),
            vmem(rows, width, dtype=F32),
            vmem(2, rows, width),
            vmem(2, rows, width),
            vmem(variables, grid_rows, dtype=F32),
            vmem(rows, width),
            pltpu.SemaphoreType.DMA((6,)),
            pltpu.SemaphoreType.DMA((chunks,)),
            pltpu.SemaphoreType.DMA((chunks,)),
            pltpu.SemaphoreType.DMA((2,)),
            pltpu.SemaphoreType.DMA((bigs,)),
            pltpu.SemaphoreType.DMA((2,)),
            pltpu.SemaphoreType.DMA((2,)),
            pltpu.SemaphoreType.DMA((2,)),
            pltpu.SemaphoreType.DMA((2,)),
        ],
        compiler_params=pltpu.CompilerParams(
            collective_id=0, has_side_effects=True, vmem_limit_bytes=56 * 2**20
        ),
        cost_estimate=pl.CostEstimate(
            flops=7_000_000_000, bytes_accessed=11_000_000, transcendentals=1_000_000
        ),
    )(
        sender_ids.T,
        block_count,
        mesh_latent,
        grid_latent,
        edge_tiles,
        w_send,
        w_grid,
        w_agg,
        w_out,
        cotangent,
    )
    return pl.pallas_call(
        finish,
        out_shape=(
            jax.ShapeDtypeStruct((variables, grid_rows), F32),
            jax.ShapeDtypeStruct((rows, width), F32),
            jax.ShapeDtypeStruct((grid_rows, width), F32),
        ),
        in_specs=[anywhere] * 5,
        out_specs=(anywhere,) * 3,
        scratch_shapes=[
            vmem(variables, grid_rows, dtype=F32),
            vmem(rows, width),
            vmem(grid_rows, width),
            vmem(*square),
            vmem(*square),
            vmem(*square),
            vmem(rows, width, dtype=F32),
            vmem(grid_rows, width, dtype=F32),
            pltpu.SemaphoreType.DMA((4,)),
            pltpu.SemaphoreType.DMA((chunks,)),
            pltpu.SemaphoreType.DMA((2,)),
            pltpu.SemaphoreType.DMA((chunks,)),
        ],
        compiler_params=pltpu.CompilerParams(vmem_limit_bytes=56 * 2**20),
    )(predictions, d_mesh_pre, d_pre, w_send, w_grid)


def solution(mesh):
    placed = (
        P(("members", "lon"), None),
        P(("members", "lon"), None),
        P("lon", None, None, None),
        P("lon", None),
        P("lon"),
        P(),
        P(),
        P(),
        P(),
        P("members", "lon"),
    )
    return jax.shard_map(
        per_device,
        mesh=mesh,
        in_specs=placed,
        out_specs=(P("members", "lon"), P(("members", "lon"), None), P(("members", "lon"), None)),
        check_vma=False,
    )
```

```python
import functools

import jax
import jax.numpy as jnp
from jax import lax
from jax.experimental import pallas as pl
from jax.experimental.pallas import tpu as pltpu
from jax.sharding import PartitionSpec as P

MESH = pl.DeviceIdType.MESH
F32 = jnp.float32
BF16 = jnp.bfloat16


def gate_of(value):
    return 0.5 * jnp.tanh(0.5 * value) + 0.5


def matmul(a, b):
    return jnp.dot(a, b, preferred_element_type=F32)


def kernel(
    lanes,
    ids_ref,
    count_ref,
    mesh_hbm,
    grid_hbm,
    tiles_hbm,
    w_send_hbm,
    w_grid_hbm,
    w_agg_hbm,
    w_out_hbm,
    cot_hbm,
    pred_hbm,
    dmesh_hbm,
    dpre_hbm,
    mesh_v,
    grid_v,
    tiles_v,
    w_send_v,
    w_grid_v,
    w_agg_v,
    w_out_v,
    cot_v,
    w_agg_t,
    mesh_pre_v,
    wide_v,
    dense_v,
    dense_t,
    part_v,
    pre_v,
    dhid_v,
    hidden_v,
    dpre_v,
    dagg_v,
    own_v,
    tx_v,
    rx_v,
    pred_v,
    dmesh_v,
    in_sem,
    grid_sem,
    tile_sem,
    out_sem,
    gout_sem,
    fsend_sem,
    frecv_sem,
    bsend_sem,
    brecv_sem,
):
    me = lax.axis_index("lon")
    odd = lax.rem(me, 2)
    far = lax.rem(me + lanes - 1 + 2 * odd, lanes)
    near = lax.rem(me + lanes + 1 - 2 * odd, lanes)
    rows = mesh_v.shape[0]
    recv, slots, side, _ = tiles_v.shape
    grid_rows = grid_v.shape[0]
    own = rows // side
    total = own * lanes
    chunk = 2 * side
    chunks = grid_rows // chunk
    big = 4 * side
    bigs = grid_rows // big

    barrier = pltpu.get_barrier_semaphore()
    for neighbour in (far, near):
        pl.semaphore_signal(barrier, inc=1, device_id={"lon": neighbour}, device_id_type=MESH)

    def load(at, src, dst):
        return pltpu.make_async_copy(src, dst, in_sem.at[at])

    loads = [
        load(0, mesh_hbm, mesh_v),
        load(1, w_send_hbm, w_send_v),
        load(2, w_grid_hbm, w_grid_v),
        load(3, w_agg_hbm, w_agg_v),
        load(4, w_out_hbm, w_out_v),
        load(5, cot_hbm, cot_v),
    ]

    def grid_copy(c):
        at = pl.ds(c * chunk, chunk)
        return pltpu.make_async_copy(grid_hbm.at[at], grid_v.at[at], grid_sem.at[c])

    def tile_copy(c):
        at = pl.ds(c * 2, 2)
        return pltpu.make_async_copy(tiles_hbm.at[at], tiles_v.at[at], tile_sem.at[c])

    for c in loads:
        c.start()
    for c in range(chunks):
        grid_copy(c).start()
        tile_copy(c).start()

    loads[0].wait()
    loads[1].wait()
    mesh_pre = matmul(mesh_v[...], w_send_v[...])
    mesh_pre_v[...] = mesh_pre
    wide_v[pl.ds(rows, rows), :] = (mesh_pre * gate_of(mesh_pre)).astype(BF16)

    pl.semaphore_wait(barrier, 2)

    rows_at = lambda start: pl.ds(pl.multiple_of(start, rows), rows)
    far_at, near_at = rows_at(odd * 2 * rows), rows_at((1 - odd) * 2 * rows)

    def halo(way):
        target, dst = (far, near_at) if way == 0 else (near, far_at)
        return pltpu.make_async_remote_copy(
            src_ref=wide_v.at[pl.ds(rows, rows)],
            dst_ref=wide_v.at[dst],
            send_sem=fsend_sem.at[way],
            recv_sem=frecv_sem.at[way],
            device_id={"lon": target},
            device_id_type=MESH,
        )

    halos = [halo(0), halo(1)]
    for copy in halos:
        copy.start()

    for c in loads[2:]:
        c.wait()
    w_agg_t[...] = w_agg_v[...].T

    halos[1].wait_recv()
    sub = 32

    def early(c, carry):
        grid_copy(c).wait()
        tile_copy(c).wait()
        at = pl.ds(pl.multiple_of(c * chunk, chunk), chunk)
        for q in range(2):
            r = c * 2 + q
            rel = []
            for k in range(slots):
                raw = lax.rem(ids_ref[k, r] - me * own + own + total, total)
                rel.append(jnp.where(k < count_ref[r], raw, -1))
            row0 = pl.multiple_of(r * side, side)
            for s in range(side // sub):
                sums = [None] * (3 * own)
                for k in range(slots):
                    tile = tiles_v[r, k, pl.ds(s * sub, sub), :].astype(F32)
                    for j in range(3 * own):
                        term = tile * jnp.where(rel[k] == j, 1.0, 0.0).astype(F32)
                        sums[j] = term if sums[j] is None else sums[j] + term
                for j in range(3 * own):
                    dense_v[pl.ds(row0 + s * sub, sub), j * side : (j + 1) * side] = sums[
                        j
                    ].astype(BF16)
            for j in range(3 * own):
                block = dense_v[pl.ds(row0, side), j * side : (j + 1) * side]
                dense_t[j * side : (j + 1) * side, pl.ds(row0, side)] = block.T
        pre_v[at, :] = matmul(grid_v[at, :], w_grid_v[...])
        dhid_v[at, :] = lax.dot_general(
            cot_v[:, at], w_out_v[...], (((0,), (0,)), ((), ())), preferred_element_type=F32
        )
        part_v[at, :] = matmul(dense_v[at, rows : 2 * rows], wide_v[rows : 2 * rows, :]) + matmul(
            dense_v[at, near_at], wide_v[near_at, :]
        )
        return carry

    lax.fori_loop(0, chunks, early, 0)

    halos[0].wait_recv()

    def dpre_copy(c):
        at = pl.ds(c * big, big)
        return pltpu.make_async_copy(dpre_v.at[at], dpre_hbm.at[at], gout_sem.at[c])

    def middle(c, carry):
        at = pl.ds(c * big, big)
        agg = part_v[at, :] + matmul(dense_v[at, far_at], wide_v[far_at, :])
        pre = pre_v[at, :] + matmul(agg.astype(BF16), w_agg_v[...])
        gate = gate_of(pre)
        hidden_v[at, :] = (pre * gate).astype(BF16)
        d_pre = (dhid_v[at, :] * (gate * (1.0 + pre * (1.0 - gate)))).astype(BF16)
        dpre_v[at, :] = d_pre
        dpre_copy(c).start()
        dagg_v[at, :] = matmul(d_pre, w_agg_t[...]).astype(BF16)
        return carry

    for c in range(bigs):
        middle(c, 0)

    def rim(way):
        target = far if way == 0 else near
        return pltpu.make_async_remote_copy(
            src_ref=tx_v.at[way],
            dst_ref=rx_v.at[way],
            send_sem=bsend_sem.at[way],
            recv_sem=brecv_sem.at[way],
            device_id={"lon": target},
            device_id_type=MESH,
        )

    rims = [rim(0), rim(1)]
    for way, side_at in ((0, far_at), (1, near_at)):
        tx_v[way] = matmul(dense_t[side_at, :], dagg_v[...]).astype(BF16)
        rims[way].start()
    own_v[...] = matmul(dense_t[rows : 2 * rows, :], dagg_v[...])

    def late(c, carry):
        at = pl.ds(pl.multiple_of(c * big, big), big)
        pred_v[:, at] = lax.dot_general(
            w_out_v[...], hidden_v[at, :], (((1,), (1,)), ((), ())), preferred_element_type=F32
        )
        return carry

    lax.fori_loop(0, bigs, late, 0)
    pred_copy = pltpu.make_async_copy(pred_v, pred_hbm, out_sem.at[0])
    pred_copy.start()

    mesh_pre = mesh_pre_v[...]
    gate = gate_of(mesh_pre)
    slope = gate * (1.0 + mesh_pre * (1.0 - gate))
    for copy in rims:
        copy.wait_recv()
    d_sender = own_v[...] + (rx_v[0].astype(F32) + rx_v[1].astype(F32))
    dmesh_v[...] = (d_sender * slope).astype(BF16)
    dmesh_copy = pltpu.make_async_copy(dmesh_v, dmesh_hbm, out_sem.at[1])
    dmesh_copy.start()

    for copy in halos + rims:
        copy.wait_send()
    for c in range(bigs):
        dpre_copy(c).wait()
    pred_copy.wait()
    dmesh_copy.wait()


def finish(
    pred_hbm,
    dmesh_hbm,
    dpre_hbm,
    w_send_hbm,
    w_grid_hbm,
    pred_out,
    gmesh_out,
    ggrid_out,
    pred_v,
    dmesh_v,
    dpre_v,
    w_send_v,
    w_grid_v,
    w_grid_t,
    gmesh_v,
    ggrid_v,
    in_sem,
    dpre_sem,
    out_sem,
    gout_sem,
):
    last = (((1,), (1,)), ((), ()))
    parts = dpre_sem.shape[0]
    step = dpre_v.shape[0] // parts

    w_grid_copy = pltpu.make_async_copy(w_grid_hbm, w_grid_v, in_sem.at[0])
    dmesh_copy = pltpu.make_async_copy(dmesh_hbm, dmesh_v, in_sem.at[1])
    w_send_copy = pltpu.make_async_copy(w_send_hbm, w_send_v, in_sem.at[2])
    pred_read = pltpu.make_async_copy(pred_hbm, pred_v, in_sem.at[3])
    pred_copy = pltpu.make_async_copy(pred_v, pred_out, out_sem.at[0])
    gmesh_copy = pltpu.make_async_copy(gmesh_v, gmesh_out, out_sem.at[1])
    reads, writes = [], []
    for c in range(parts):
        at = pl.ds(c * step, step)
        reads.append(pltpu.make_async_copy(dpre_hbm.at[at], dpre_v.at[at], dpre_sem.at[c]))
        writes.append(pltpu.make_async_copy(ggrid_v.at[at], ggrid_out.at[at], gout_sem.at[c]))
    w_grid_copy.start()
    for copy in reads:
        copy.start()
    dmesh_copy.start()
    w_send_copy.start()
    pred_read.start()
    w_grid_copy.wait()
    w_grid_t[...] = w_grid_v[...].T
    for c in range(parts):
        at = pl.ds(c * step, step)
        reads[c].wait()
        ggrid_v[at, :] = matmul(dpre_v[at, :], w_grid_t[...])
        writes[c].start()
    pred_read.wait()
    pred_copy.start()
    dmesh_copy.wait()
    w_send_copy.wait()
    gmesh_v[...] = lax.dot_general(dmesh_v[...], w_send_v[...], last, preferred_element_type=F32)
    gmesh_copy.start()
    for copy in writes:
        copy.wait()
    pred_copy.wait()
    gmesh_copy.wait()


def per_device(
    mesh_latent,
    grid_latent,
    edge_tiles,
    sender_ids,
    block_count,
    w_send,
    w_grid,
    w_agg,
    w_out,
    cotangent,
):
    lanes = lax.axis_size("lon")
    rows, width = mesh_latent.shape
    grid_rows = grid_latent.shape[0]
    recv, _, side, _ = edge_tiles.shape
    variables = w_out.shape[0]
    wide = 3 * rows
    anywhere = pl.BlockSpec(memory_space=pl.ANY)
    scalars = pl.BlockSpec(memory_space=pltpu.SMEM)
    chunks = recv // 2
    bigs = recv // 4

    def vmem(*shape, dtype=BF16):
        return pltpu.VMEM(shape, dtype)

    square = (width, width)
    predictions, d_mesh_pre, d_pre = pl.pallas_call(
        functools.partial(kernel, lanes),
        out_shape=(
            jax.ShapeDtypeStruct((variables, grid_rows), F32),
            jax.ShapeDtypeStruct((rows, width), BF16),
            jax.ShapeDtypeStruct((grid_rows, width), BF16),
        ),
        in_specs=[scalars] * 2 + [anywhere] * 8,
        out_specs=(anywhere,) * 3,
        scratch_shapes=[
            vmem(rows, width),
            vmem(grid_rows, width),
            vmem(*edge_tiles.shape),
            vmem(*square),
            vmem(*square),
            vmem(*square),
            vmem(variables, width),
            vmem(variables, grid_rows),
            vmem(*square),
            vmem(rows, width, dtype=F32),
            vmem(wide, width),
            vmem(grid_rows, wide),
            vmem(wide, grid_rows),
            vmem(grid_rows, width, dtype=F32),
            vmem(grid_rows, width, dtype=F32),
            vmem(grid_rows, width, dtype=F32),
            vmem(grid_rows, width),
            vmem(grid_rows, width),
            vmem(grid_rows, width),
            vmem(rows, width, dtype=F32),
            vmem(2, rows, width),
            vmem(2, rows, width),
            vmem(variables, grid_rows, dtype=F32),
            vmem(rows, width),
            pltpu.SemaphoreType.DMA((6,)),
            pltpu.SemaphoreType.DMA((chunks,)),
            pltpu.SemaphoreType.DMA((chunks,)),
            pltpu.SemaphoreType.DMA((2,)),
            pltpu.SemaphoreType.DMA((bigs,)),
            pltpu.SemaphoreType.DMA((2,)),
            pltpu.SemaphoreType.DMA((2,)),
            pltpu.SemaphoreType.DMA((2,)),
            pltpu.SemaphoreType.DMA((2,)),
        ],
        compiler_params=pltpu.CompilerParams(
            collective_id=0, has_side_effects=True, vmem_limit_bytes=56 * 2**20
        ),
        cost_estimate=pl.CostEstimate(
            flops=7_000_000_000, bytes_accessed=11_000_000, transcendentals=1_000_000
        ),
    )(
        sender_ids.T,
        block_count,
        mesh_latent,
        grid_latent,
        edge_tiles,
        w_send,
        w_grid,
        w_agg,
        w_out,
        cotangent,
    )
    return pl.pallas_call(
        finish,
        out_shape=(
            jax.ShapeDtypeStruct((variables, grid_rows), F32),
            jax.ShapeDtypeStruct((rows, width), F32),
            jax.ShapeDtypeStruct((grid_rows, width), F32),
        ),
        in_specs=[anywhere] * 5,
        out_specs=(anywhere,) * 3,
        scratch_shapes=[
            vmem(variables, grid_rows, dtype=F32),
            vmem(rows, width),
            vmem(grid_rows, width),
            vmem(*square),
            vmem(*square),
            vmem(*square),
            vmem(rows, width, dtype=F32),
            vmem(grid_rows, width, dtype=F32),
            pltpu.SemaphoreType.DMA((4,)),
            pltpu.SemaphoreType.DMA((chunks,)),
            pltpu.SemaphoreType.DMA((2,)),
            pltpu.SemaphoreType.DMA((chunks,)),
        ],
        compiler_params=pltpu.CompilerParams(vmem_limit_bytes=56 * 2**20),
    )(predictions, d_mesh_pre, d_pre, w_send, w_grid)


def solution(mesh):
    placed = (
        P(("members", "lon"), None),
        P(("members", "lon"), None),
        P("lon", None, None, None),
        P("lon", None),
        P("lon"),
        P(),
        P(),
        P(),
        P(),
        P("members", "lon"),
    )
    return jax.shard_map(
        per_device,
        mesh=mesh,
        in_specs=placed,
        out_specs=(P("members", "lon"), P(("members", "lon"), None), P(("members", "lon"), None)),
        check_vma=False,
    )
```
